128 devices in a mesh: dp: 16 (over y_hi, x, core), mp: 8 (over z, y_lo).
Axes of the slice: x: 4, y: 4 (y_hi: 2, y_lo: 2; y = y_hi * 2 + y_lo), z: 4, core: 2. Of those that a mesh axis runs over, the one named last changes fastest.
Arguments:
- acts: bfloat16 [2048, 4608], P('dp', 'mp'), may hold values from -6 to 6
- old_weights: bfloat16 [2, 4608, 18432], P(None, ('mp', 'dp')), may hold values from -4 to 4
- old_mean: bfloat16 [2, 4608, 18432], P(None, ('mp', 'dp')), may hold values from -2 to 2
- old_var: float32 [2, 4608, 18432], P(None, ('mp', 'dp')), may hold values from 0.05 to 0.5
- cotangent: bfloat16 [2048, 18432], P('mp', 'dp'), may hold values from -6 to 6
Outputs:
- hidden: bfloat16 [2048, 18432], P('mp', 'dp')
- input_grad: bfloat16 [2048, 4608], P('dp', 'mp')
- new_weights: bfloat16 [2, 4608, 18432], P(None, 'mp', 'dp')
- new_mean: bfloat16 [2, 4608, 18432], P(None, 'mp', 'dp')
- new_var: float32 [2, 4608, 18432], P(None, 'mp', 'dp')
The draws below stay inside these ranges and needn't reach their ends.
All inputs are finite; a program needn't handle non-finite values.
Results may differ from the reference program's by a relative error of at most 0.005.
Values may be sent and summed in bfloat16 or wider, within the bound.
A program may use at most 192 MiB of HBM per device.

```python
import math
import jax
import jax.numpy as jnp

D = 4608
FFW = 18432
RESUME_STEP = 1000
TOKENS = 2048


def spiked(values, stream_key, source, target, parts, factor):
    owner, partner = [(jnp.arange(values.shape[position]) // (values.shape[position] // parts)).reshape([-1 if axis == position else 1 for axis in range(values.ndim)]) for position in (source, target)]
    chosen = jax.random.permutation(stream_key, parts)[partner]
    strong = (owner == chosen) | (owner == (partner + parts // 2) % parts)
    return jnp.where(strong, factor * values, values)


def shard_levels(own_key, dims, cuts, smallest, high):
    level = 1.0
    for position, shards_of in cuts:
        steps = jax.random.uniform(jax.random.fold_in(jax.random.fold_in(own_key, 6), position), (shards_of,), jnp.float32, smallest / len(cuts), high / len(cuts))
        level = level * jnp.repeat(jnp.exp(steps), dims[position] // shards_of).reshape((-1,) + (1,) * (len(dims) - 1 - position))
    return level


def bell_draw(key, extent, scale, limit, split=(), held_as=jnp.bfloat16):
    drawn = scale * jax.random.normal(key, extent, jnp.float32)
    if split:
        drawn = drawn * shard_levels(key, extent, split, -0.22, 0.18)
    return jnp.clip(drawn, -limit, limit).astype(held_as)


def bell_draw_with(key, dims, spread, most, cuts, heavy, dtype=jnp.bfloat16):
    values = spread * jax.random.normal(key, dims, jnp.float32)
    if cuts:
        values = values * shard_levels(key, dims, cuts, -0.22, 0.18)
    return jnp.clip(spiked(values, jax.random.fold_in(key, 3), *heavy), -most, most).astype(dtype)


def setup_inputs(seed: int = 0) -> dict:
    key_list = jax.random.split(jax.random.key(seed), 6)
    acts = bell_draw(key_list[0], (TOKENS, D), 1.0, 6.0, ((0, 16), (1, 8)))
    old_weights = bell_draw(key_list[1], (2, D, FFW), 1.0, 4.0, ((1, 128),))
    old_mean = bell_draw(key_list[2], (2, D, FFW), 0.3, 2.0, ((1, 128),))
    old_var = jnp.clip(jnp.exp(math.log(0.5) - 2.3025851 * jax.random.uniform(key_list[3], (2, D, FFW), jnp.float32) ** shard_levels(key_list[3], (2, D, FFW), ((1, 128),), -0.2, 0.2)), 0.05, 0.5)
    cotangent = bell_draw_with(key_list[4], (TOKENS, FFW), 1.0, 6.0, ((0, 8), (1, 16)), (1, 0, 16, 2.0))
    return dict(acts=acts, old_weights=old_weights, old_mean=old_mean, old_var=old_var, cotangent=cotangent)


tanh_coef = 0.7978845608028654
cube_coef = 0.044715
beta_one = 0.9
beta_two = 0.95
learn_rate = 0.05
decay_rate = 0.1
epsilon = 1e-08

def gelu_value(value):
    return 0.5 * value * (1.0 + jnp.tanh(tanh_coef * (value + cube_coef * value * value * value)))

def gelu_slope(value):
    inner = jnp.tanh(tanh_coef * (value + cube_coef * value * value * value))
    return 0.5 * (1.0 + inner) + 0.5 * value * (1.0 - inner * inner) * tanh_coef * (1.0 + 3.0 * cube_coef * value * value)

def adam_update(weights, mean, variance, weight_grads):
    moment_one = beta_one * mean.astype(jnp.float32) + (1.0 - beta_one) * weight_grads
    var_next = beta_two * variance + (1.0 - beta_two) * weight_grads * weight_grads
    mean_hat = moment_one / (1.0 - beta_one ** RESUME_STEP)
    var_hat = var_next / (1.0 - beta_two ** RESUME_STEP)
    master = weights.astype(jnp.float32)
    updated = master - learn_rate * (mean_hat / (jnp.sqrt(var_hat) + epsilon) + decay_rate * master)
    return (updated.astype(jnp.bfloat16), moment_one.astype(jnp.bfloat16), var_next)

def reference(acts, old_weights, old_mean, old_var, cotangent):
    width_scale = D ** (-0.5)
    gate = jnp.dot(acts, old_weights[0], preferred_element_type=jnp.float32) * width_scale
    up_proj = jnp.dot(acts, old_weights[1], preferred_element_type=jnp.float32) * width_scale
    activated = gelu_value(gate)
    hidden = (activated * up_proj).astype(jnp.bfloat16)
    upstream = cotangent.astype(jnp.float32)
    gate_grad = (upstream * up_proj * gelu_slope(gate)).astype(jnp.bfloat16)
    up_grad = (upstream * activated).astype(jnp.bfloat16)
    grad_first = jnp.dot(acts.T, gate_grad, preferred_element_type=jnp.float32) * width_scale
    grad_second = jnp.dot(acts.T, up_grad, preferred_element_type=jnp.float32) * width_scale
    weight_grads = jnp.stack([grad_first, grad_second])
    back_sum = jnp.dot(gate_grad, old_weights[0].T, preferred_element_type=jnp.float32)
    back_sum = back_sum + jnp.dot(up_grad, old_weights[1].T, preferred_element_type=jnp.float32)
    input_grad = (back_sum * width_scale).astype(jnp.bfloat16)
    new_weights, new_mean, new_var = adam_update(old_weights, old_mean, old_var, weight_grads)
    return (hidden, input_grad, new_weights, new_mean, new_var)
```

```python
import functools

import jax
import jax.numpy as jnp
from jax import lax
from jax.experimental import pallas as pl
from jax.experimental.pallas import tpu as pltpu
from jax.sharding import PartitionSpec as P

D = 4608
RESUME_STEP = 1000

tanh_coef = 0.7978845608028654
cube_coef = 0.044715
beta_one = 0.9
beta_two = 0.95
learn_rate = 0.05
decay_rate = 0.1
epsilon = 1e-08
width_scale = D ** (-0.5)

MESH = pl.DeviceIdType.MESH
F32 = jnp.float32
BF16 = jnp.bfloat16

DP, Z, LO = 16, 4, 2
ROWS = 36
WIDTH = ROWS * DP
TOK = 2048
BLOCK = TOK // Z
HALF = BLOCK // LO
FS = 1152
CH = 3
FC = FS // CH
OWN = TOK // DP


def gelu_parts(value):
    inner = jnp.tanh(tanh_coef * (value + cube_coef * value * value * value))
    activated = 0.5 * value * (1.0 + inner)
    slope = 0.5 * (1.0 + inner) + 0.5 * value * (1.0 - inner * inner) * tanh_coef * (
        1.0 + 3.0 * cube_coef * value * value
    )
    return activated, slope


def dot(left, right):
    return jnp.dot(left, right, preferred_element_type=F32)


def kernel(
    at_in, w_in, m_in, v_in, cot, hid, ig, nw, nm, nv,
    at, a, wr, mr, vr, wd, sb, rmid, rfin, yls, ylr, grads, acc, gw, nws, nms, nvs, xs, xr, xf,
    copy_sem, out_sem, act_send, act_recv, fwd_send, fwd_recv, rel_send, rel_recv,
    zs_sem, zr_sem, x_send, x_recv,
):
    dp, mp = lax.axis_index("dp"), lax.axis_index("mp")
    core = lax.rem(dp, 2)
    line = lax.div(dp, 2)
    x = lax.rem(line, 4)
    y_hi = lax.div(line, 4)
    z = lax.div(mp, 2)
    lo = lax.rem(mp, 2)

    def z_dev(step):
        return (dp, lax.rem(z + step, Z) * 2 + lo)

    plus, minus = z_dev(1), z_dev(Z - 1)
    mate = (dp, z * 2 + 1 - lo)
    twin = (dp + 1 - 2 * core, mp)

    def peer_dp(i):
        far = 1 - lax.rem(i, 2)
        j = lax.div(i, 2) + lax.rem(i, 2)
        q = lax.div(j, 2)
        step = q + lax.div(q, 2) * (1 - 2 * lax.rem(q, 2))
        other = lax.rem(core + lax.rem(j, 2), 2)
        return lax.rem(y_hi + far, 2) * 8 + lax.rem(x + step, 4) * 2 + other

    def peer_line(i):
        far = lax.rem(i, 2)
        q = lax.div(i, 2)
        step = q + lax.div(q, 2) * (1 - 2 * lax.rem(q, 2))
        return lax.rem(y_hi + far, 2) * 4 + lax.rem(x + step, 4)

    barrier = pltpu.get_barrier_semaphore()

    @pl.loop(0, DP - 1)
    def _(i):
        pl.semaphore_signal(barrier, inc=1, device_id=(peer_dp(i), mp), device_id_type=MESH)

    for other in (plus, minus, mate):
        pl.semaphore_signal(barrier, inc=1, device_id=other, device_id_type=MESH)
    pl.semaphore_wait(barrier, DP - 1 + 3)

    def remote(src, dst, send, recv, device):
        return pltpu.make_async_remote_copy(
            src_ref=src, dst_ref=dst, send_sem=send, recv_sem=recv, device_id=device, device_id_type=MESH
        )

    def cols(index):
        return pl.ds(pl.multiple_of(index * OWN, OWN), OWN)

    own_act = pltpu.make_async_copy(at_in, at.at[:, cols(dp)], copy_sem)
    own_act.start()

    @pl.loop(1, 8)
    def _(i):
        remote(at_in, at.at[:, cols(dp)], act_send, act_recv.at[i - 1], (peer_line(i) * 2 + core, mp)).start()

    remote(at_in, at.at[:, cols(dp)], fwd_send, fwd_recv, twin).start()

    def relay(index, src, dst, c):
        mine = pl.ds(dp * ROWS, ROWS)

        def part(owner):
            return src.at[:, :, pl.ds(pl.multiple_of(owner * FS + c * FC, 128), FC)]

        pltpu.make_async_copy(part(dp), dst.at[c, mine], rel_recv.at[index, c]).start()

        @pl.loop(0, DP - 1)
        def _(i):
            owner = peer_dp(i)
            remote(part(owner), dst.at[c, mine], rel_send.at[index, c], rel_recv.at[index, c], (owner, mp)).start()

    def relayed(index, dst, c):
        pltpu.make_async_copy(dst.at[c], dst.at[c], rel_recv.at[index, c]).wait()

    def relay_sent(index, dst, c):
        sent = dst.at[c, pl.ds(0, WIDTH - ROWS)]
        pltpu.make_async_copy(sent, sent, rel_send.at[index, c]).wait()

    for c in range(CH):
        relay(0, w_in, wr, c)

    own_act.wait()

    @pl.loop(1, 8)
    def _(i):
        far = lax.rem(i, 2)
        q = lax.div(i, 2)
        step = q + lax.div(q, 2) * (1 - 2 * lax.rem(q, 2))
        source = (lax.rem(y_hi + far, 2) * 4 + lax.rem(x + 4 - step, 4)) * 2 + core
        block = at.at[:, cols(source)]
        remote(block, block, act_send, act_recv.at[i - 1], twin).wait_recv()
        remote(block, block, fwd_send, fwd_recv, twin).start()

    half_acts = at.at[:, pl.ds(0, TOK // 2)]
    pltpu.make_async_copy(half_acts, half_acts, fwd_recv).wait()

    @pl.loop(0, DP)
    def _(i):
        a[pl.ds(pl.multiple_of(i * OWN, OWN), OWN), :] = at[:, cols(i)].T

    def tokens(step, half):
        return pl.ds(pl.multiple_of(lax.rem(z + step, Z) * BLOCK + half * HALF, HALF), HALF)

    sends = []

    def zsend(c, slot, src, dst, device):
        copy = remote(src, dst, zs_sem.at[c, slot], zr_sem.at[c, slot], device)
        copy.start()
        sends.append(copy)

    def zwait(c, slot, dst):
        remote(dst, dst, zs_sem.at[c, slot], zr_sem.at[c, slot], plus).wait_recv()

    def first(c):
        relayed(0, wr, c)

        @pl.loop(0, WIDTH // 32)
        def _(i):
            rows = pl.ds(pl.multiple_of(i * 32, 32), 32)
            pair = jnp.swapaxes(wr[c, rows], 0, 1)
            wd[c, rows, 0:FC] = pair[0]
            wd[c, rows, FC : 2 * FC] = pair[1]

        @pl.loop(0, 4)
        def _(slot):
            late = lax.div(slot, 2)
            odd = lax.rem(slot, 2)
            step = 2 + late * (2 * odd - 1)
            half = odd + late * (1 - 2 * odd)
            sb[c, slot] = dot(a[tokens(step, half), :], wd[c]).astype(BF16)

        zsend(c, 0, sb.at[c, 0], rmid.at[c, 0], plus)
        zsend(c, 1, sb.at[c, 1], rmid.at[c, 1], minus)
        zsend(c, 2, sb.at[c, 2], rfin.at[c, 0, 1], plus)
        zsend(c, 3, sb.at[c, 3], rfin.at[c, 1, 0], minus)

    def second(c):
        zwait(c, 0, rmid.at[c, 0])
        zwait(c, 1, rmid.at[c, 1])

        @pl.loop(0, 2)
        def _(slot):
            sb[c, 4 + slot] = (
                dot(a[tokens(1 + 2 * slot, slot), :], wd[c]) + rmid[c, slot].astype(F32)
            ).astype(BF16)

        zsend(c, 4, sb.at[c, 4], rfin.at[c, 0, 0], plus)
        zsend(c, 5, sb.at[c, 5], rfin.at[c, 1, 1], minus)

    def block_sum(c, half):
        return (
            dot(a[tokens(0, half), :], wd[c])
            + rfin[c, 0, half].astype(F32)
            + rfin[c, 1, half].astype(F32)
        )

    def third(c):
        zwait(c, 2, rfin.at[c, 0, 1])
        zwait(c, 3, rfin.at[c, 1, 0])
        zwait(c, 4, rfin.at[c, 0, 0])
        zwait(c, 5, rfin.at[c, 1, 1])
        yls[c] = block_sum(c, 1 - lo).astype(BF16)
        zsend(c, 6, yls.at[c], ylr.at[c], mate)

    def fourth(c):
        zwait(c, 6, ylr.at[c])
        sums = (block_sum(c, lo) + ylr[c].astype(F32)) * width_scale
        gate, up = sums[:, :FC], sums[:, FC:]
        span = slice(c * FC, (c + 1) * FC)
        activated, slope = gelu_parts(gate)
        upstream = cot[:, span].astype(F32)
        hid[:, span] = (activated * up).astype(BF16)
        rows = tokens(0, lo)
        grads[c, rows, 0:FC] = (upstream * up * slope).astype(BF16)
        grads[c, rows, FC : 2 * FC] = (upstream * activated).astype(BF16)
        mine = grads.at[c, rows]
        zsend(c, 7, mine, mine, mate)
        zsend(c, 8, mine, mine, plus)
        zsend(c, 9, mine, mine, minus)

    def fifth(c):
        theirs = grads.at[c, tokens(0, 1 - lo)]
        zwait(c, 7, theirs)
        zsend(c, 10, theirs, theirs, plus)
        zsend(c, 11, theirs, theirs, minus)

    def sixth(c):
        below, above = grads.at[c, tokens(3, lo)], grads.at[c, tokens(1, 1 - lo)]
        zwait(c, 8, below)
        zsend(c, 12, below, below, plus)
        zwait(c, 11, above)
        zsend(c, 13, above, above, minus)

    def gathered(c):
        zwait(c, 9, grads.at[c, tokens(1, lo)])
        zwait(c, 10, grads.at[c, tokens(3, 1 - lo)])
        zwait(c, 12, grads.at[c, tokens(2, lo)])
        zwait(c, 13, grads.at[c, tokens(2, 1 - lo)])

    def back(c):
        @pl.loop(0, TOK // HALF)
        def _(i):
            rows = pl.ds(pl.multiple_of(i * HALF, HALF), HALF)
            term = lax.dot_general(
                grads[c, rows, :], wd[c], (((1,), (1,)), ((), ())), preferred_element_type=F32
            )
            if c == 0:
                acc[rows, :] = term
            else:
                acc[rows, :] += term

    outs = ((nws, nw), (nms, nm), (nvs, nv))

    def written(c):
        span = pl.ds(c * FC, FC)
        return [
            pltpu.make_async_copy(held, out.at[:, :, span], out_sem.at[i]) for i, (held, out) in enumerate(outs)
        ]

    def weight_grads(c):
        @pl.loop(0, 6)
        def _(i):
            k = lax.rem(i, 2)
            rows = pl.ds(pl.multiple_of(lax.div(i, 2) * 192, 192), 192)
            span = pl.ds(pl.multiple_of(k * FC, FC), FC)
            gw[k, rows, :] = dot(at[rows, :], grads[c, :, span]) * width_scale

    def update(c):
        relayed(1, mr, c)
        relayed(2, vr, c)
        if c > 0:
            for copy in written(c - 1):
                copy.wait()

        @pl.loop(0, WIDTH // 32)
        def _(i):
            rows = pl.ds(pl.multiple_of(i * 32, 32), 32)
            mean = jnp.swapaxes(mr[c, rows], 0, 1)
            var = jnp.swapaxes(vr[c, rows], 0, 1)
            for k in range(2):
                grad = gw[k, rows, :]
                moment_one = beta_one * mean[k].astype(F32) + (1.0 - beta_one) * grad
                var_next = beta_two * var[k].astype(F32) + (1.0 - beta_two) * grad * grad
                mean_hat = moment_one / (1.0 - beta_one**RESUME_STEP)
                var_hat = var_next / (1.0 - beta_two**RESUME_STEP)
                master = wd[c, rows, k * FC : (k + 1) * FC].astype(F32)
                updated = master - learn_rate * (
                    mean_hat / (jnp.sqrt(var_hat) + epsilon) + decay_rate * master
                )
                nws[k, rows, :] = updated.astype(BF16)
                nms[k, rows, :] = moment_one.astype(BF16)
                nvs[k, rows, :] = var_next

        for copy in written(c):
            copy.start()

    first(0)
    relay(1, m_in, mr, 0)
    first(1)
    second(0)
    relay(2, v_in, vr, 0)
    first(2)
    second(1)
    relay(1, m_in, mr, 1)
    third(0)
    fourth(0)
    second(2)
    relay(2, v_in, vr, 1)
    fifth(0)
    third(1)
    fourth(1)
    relay(1, m_in, mr, 2)
    sixth(0)
    fifth(1)
    third(2)
    fourth(2)
    relay(2, v_in, vr, 2)
    gathered(0)
    fifth(2)
    sixth(1)
    back(0)
    weight_grads(0)
    update(0)
    sixth(2)
    gathered(1)
    back(1)
    weight_grads(1)
    update(1)
    gathered(2)
    back(2)

    def acc_rows(index):
        return pl.ds(pl.multiple_of(index * OWN, OWN), OWN)

    @pl.loop(0, 8)
    def _(j):
        xs[j] = acc[acc_rows(j * 2 + 1 - core), :].astype(BF16)

    swap = remote(xs, xr, x_send.at[0], x_recv.at[0], twin)
    swap.start()
    weight_grads(2)
    swap.wait()

    @pl.loop(0, 8)
    def _(j):
        rows = acc_rows(j * 2 + core)
        total = acc[rows, :] + xr[j].astype(F32)
        acc[rows, :] = total
        xs[j] = total.astype(BF16)

    @pl.loop(1, 8)
    def _(i):
        owner = peer_line(i)
        remote(xs.at[owner], xf.at[i - 1], x_send.at[1], x_recv.at[1], (owner * 2 + core, mp)).start()

    update(2)
    pltpu.make_async_copy(xf, xf, x_recv.at[1]).wait()
    total = acc[acc_rows(dp), :]
    for i in range(7):
        total = total + xf[i].astype(F32)
    ig[...] = (total * width_scale).T.astype(BF16)

    pltpu.make_async_copy(xf, xf, x_send.at[1]).wait()
    for copy in written(CH - 1):
        copy.wait()
    for copy in sends:
        copy.wait_send()
    for c in range(CH):
        relay_sent(0, wr, c)
        relay_sent(1, mr, c)
        relay_sent(2, vr, c)
    seven = at.at[:, pl.ds(0, 7 * OWN)]
    pltpu.make_async_copy(seven, seven, act_send).wait()
    pltpu.make_async_copy(half_acts, half_acts, fwd_send).wait()


def shards(acts, old_weights, old_mean, old_var, cotangent):
    vmem = pl.BlockSpec(memory_space=pltpu.VMEM)
    hbm = pl.BlockSpec(memory_space=pl.ANY)
    dma = pltpu.SemaphoreType.DMA
    macs = 3 * TOK * WIDTH * 2 * FS

    hidden, input_grad, new_weights, new_mean, new_var = pl.pallas_call(
        kernel,
        out_shape=(
            jax.ShapeDtypeStruct((HALF, FS), BF16),
            jax.ShapeDtypeStruct((WIDTH, OWN), BF16),
            jax.ShapeDtypeStruct((2, WIDTH, FS), BF16),
            jax.ShapeDtypeStruct((2, WIDTH, FS), BF16),
            jax.ShapeDtypeStruct((2, WIDTH, FS), F32),
        ),
        in_specs=[hbm, hbm, hbm, hbm, vmem],
        out_specs=(vmem, vmem, hbm, hbm, hbm),
        scratch_shapes=[
            pltpu.VMEM((WIDTH, TOK), BF16),
            pltpu.VMEM((TOK, WIDTH), BF16),
            pltpu.VMEM((CH, WIDTH, 2, FC), BF16),
            pltpu.VMEM((CH, WIDTH, 2, FC), BF16),
            pltpu.VMEM((CH, WIDTH, 2, FC), BF16),
            pltpu.VMEM((CH, WIDTH, 2 * FC), BF16),
            pltpu.VMEM((CH, 6, HALF, 2 * FC), BF16),
            pltpu.VMEM((CH, 2, HALF, 2 * FC), BF16),
            pltpu.VMEM((CH, 2, 2, HALF, 2 * FC), BF16),
            pltpu.VMEM((CH, HALF, 2 * FC), BF16),
            pltpu.VMEM((CH, HALF, 2 * FC), BF16),
            pltpu.VMEM((CH, TOK, 2 * FC), BF16),
            pltpu.VMEM((TOK, WIDTH), F32),
            pltpu.VMEM((2, WIDTH, FC), F32),
            pltpu.VMEM((2, WIDTH, FC), BF16),
            pltpu.VMEM((2, WIDTH, FC), BF16),
            pltpu.VMEM((2, WIDTH, FC), F32),
            pltpu.VMEM((8, OWN, WIDTH), BF16),
            pltpu.VMEM((8, OWN, WIDTH), BF16),
            pltpu.VMEM((7, OWN, WIDTH), BF16),
            dma, dma((3,)), dma, dma((7,)), dma, dma, dma((3, CH)), dma((3, CH)),
            dma((CH, 14)), dma((CH, 14)), dma((2,)), dma((2,)),
        ],
        compiler_params=pltpu.CompilerParams(
            collective_id=0, has_side_effects=True, vmem_limit_bytes=63 * 2**20
        ),
        cost_estimate=pl.CostEstimate(flops=2 * macs, bytes_accessed=40 * 2**20, transcendentals=0),
    )(
        acts.T,
        jnp.transpose(old_weights, (1, 0, 2)),
        jnp.transpose(old_mean, (1, 0, 2)),
        jnp.transpose(old_var, (1, 0, 2)).astype(BF16),
        cotangent,
    )
    return hidden, input_grad.T, new_weights, new_mean, new_var


def solution(mesh):
    placed = (
        P("dp", "mp"),
        P(None, ("mp", "dp"), None),
        P(None, ("mp", "dp"), None),
        P(None, ("mp", "dp"), None),
        P("mp", "dp"),
    )
    return jax.shard_map(
        shards,
        mesh=mesh,
        in_specs=placed,
        out_specs=(
            P("mp", "dp"),
            P("dp", "mp"),
            P(None, "mp", "dp"),
            P(None, "mp", "dp"),
            P(None, "mp", "dp"),
        ),
        check_vma=False,
    )
```

```python
import functools

import jax
import jax.numpy as jnp
from jax import lax
from jax.experimental import pallas as pl
from jax.experimental.pallas import tpu as pltpu
from jax.sharding import PartitionSpec as P

D = 4608
RESUME_STEP = 1000

tanh_coef = 0.7978845608028654
cube_coef = 0.044715
beta_one = 0.9
beta_two = 0.95
learn_rate = 0.05
decay_rate = 0.1
epsilon = 1e-08
width_scale = D ** (-0.5)

MESH = pl.DeviceIdType.MESH
F32 = jnp.float32
BF16 = jnp.bfloat16

DP, Z, LO = 16, 4, 2
ROWS = 36
WIDTH = ROWS * DP
TOK = 2048
BLOCK = TOK // Z
HALF = BLOCK // LO
FS = 1152
CH = 9
FC = FS // CH
LAG = 4
PIECE = 9
OWN = TOK // DP


def gelu_parts(value):
    inner = jnp.tanh(tanh_coef * (value + cube_coef * value * value * value))
    activated = 0.5 * value * (1.0 + inner)
    slope = 0.5 * (1.0 + inner) + 0.5 * value * (1.0 - inner * inner) * tanh_coef * (
        1.0 + 3.0 * cube_coef * value * value
    )
    return activated, slope


def dot(left, right):
    return jnp.dot(left, right, preferred_element_type=F32)


def kernel(
    at_in, w_in, m_in, v_in, cot, hid, ig, nw, nm, nv,
    vf, vb, at, a, wr, mr, vr, wd, sb, rmid, rfin, yls, ylr, grads, acc, gw, nws, nms, nvs, xs, xr, xq, xf,
    copy_sem, cast_sem, out_sem, act_send, act_recv, fwd_send, fwd_recv, rel_send, rel_recv,
    zs_sem, zr_sem, x_send, x_recv, p_send, p_recv,
):
    dp, mp = lax.axis_index("dp"), lax.axis_index("mp")
    core = lax.rem(dp, 2)
    line = lax.div(dp, 2)
    x = lax.rem(line, 4)
    y_hi = lax.div(line, 4)
    z = lax.div(mp, 2)
    lo = lax.rem(mp, 2)

    def z_dev(step):
        return (dp, lax.rem(z + step, Z) * 2 + lo)

    plus, minus = z_dev(1), z_dev(Z - 1)
    mate = (dp, z * 2 + 1 - lo)
    twin = (dp + 1 - 2 * core, mp)

    def peer_dp(i):
        far = 1 - lax.rem(i, 2)
        j = lax.div(i, 2) + lax.rem(i, 2)
        q = lax.div(j, 2)
        step = q + lax.div(q, 2) * (1 - 2 * lax.rem(q, 2))
        other = lax.rem(core + lax.rem(j, 2), 2)
        return lax.rem(y_hi + far, 2) * 8 + lax.rem(x + step, 4) * 2 + other

    def peer_line(i):
        far = lax.rem(i, 2)
        q = lax.div(i, 2)
        step = q + lax.div(q, 2) * (1 - 2 * lax.rem(q, 2))
        return lax.rem(y_hi + far, 2) * 4 + lax.rem(x + step, 4)

    def cast_part(i):
        return pltpu.make_async_copy(v_in.at[pl.ds(i * PIECE, PIECE)], vf.at[i % 2], cast_sem.at[i % 2])

    cast_part(0).start()
    cast_part(1).start()

    barrier = pltpu.get_barrier_semaphore()

    @pl.loop(0, DP - 1)
    def _(i):
        pl.semaphore_signal(barrier, inc=1, device_id=(peer_dp(i), mp), device_id_type=MESH)

    for other in (plus, minus, mate):
        pl.semaphore_signal(barrier, inc=1, device_id=other, device_id_type=MESH)
    pl.semaphore_wait(barrier, DP - 1 + 3)

    def remote(src, dst, send, recv, device):
        return pltpu.make_async_remote_copy(
            src_ref=src, dst_ref=dst, send_sem=send, recv_sem=recv, device_id=device, device_id_type=MESH
        )

    def cols(index):
        return pl.ds(pl.multiple_of(index * OWN, OWN), OWN)

    own_act = pltpu.make_async_copy(at_in, at.at[:, cols(dp)], copy_sem)
    own_act.start()

    @pl.loop(1, 8)
    def _(i):
        remote(at_in, at.at[:, cols(dp)], act_send, act_recv.at[i - 1], (peer_line(i) * 2 + core, mp)).start()

    remote(at_in, at.at[:, cols(dp)], fwd_send, fwd_recv, twin).start()

    def relay(index, src, dst, c):
        mine = pl.ds(dp * ROWS, ROWS)

        def part(owner):
            return src.at[:, :, pl.ds(pl.multiple_of(owner * FS + c * FC, 128), FC)]

        pltpu.make_async_copy(part(dp), dst.at[c, mine], rel_recv.at[index, c]).start()

        @pl.loop(0, DP - 1)
        def _(i):
            owner = peer_dp(i)
            remote(part(owner), dst.at[c, mine], rel_send.at[index, c], rel_recv.at[index, c], (owner, mp)).start()

    def relayed(index, dst, c):
        pltpu.make_async_copy(dst.at[c], dst.at[c], rel_recv.at[index, c]).wait()

    def relay_sent(index, dst, c):
        sent = dst.at[c, pl.ds(0, WIDTH - ROWS)]
        pltpu.make_async_copy(sent, sent, rel_send.at[index, c]).wait()

    for c in range(2):
        relay(0, w_in, wr, c)

    for i in range(ROWS // PIECE):
        cast_part(i).wait()

        @pl.loop(0, PIECE)
        def _(row):
            vb[i * PIECE + row] = vf[i % 2, row].astype(BF16)

        if i + 2 < ROWS // PIECE:
            cast_part(i + 2).start()

    def turn(index):
        a[pl.ds(pl.multiple_of(index * OWN, OWN), OWN), :] = at[:, cols(index)].T

    own_act.wait()
    turn(dp)

    @pl.loop(1, 8)
    def _(i):
        far = lax.rem(i, 2)
        q = lax.div(i, 2)
        step = q + lax.div(q, 2) * (1 - 2 * lax.rem(q, 2))
        source = (lax.rem(y_hi + far, 2) * 4 + lax.rem(x + 4 - step, 4)) * 2 + core
        block = at.at[:, cols(source)]
        remote(block, block, act_send, act_recv.at[i - 1], twin).wait_recv()
        remote(block, block, fwd_send, fwd_recv, twin).start()
        turn(source)

    half_acts = at.at[:, pl.ds(0, TOK // 2)]
    pltpu.make_async_copy(half_acts, half_acts, fwd_recv).wait()

    @pl.loop(0, DP // 2)
    def _(i):
        turn(i * 2 + 1 - core)

    def tokens(step, half):
        return pl.ds(pl.multiple_of(lax.rem(z + step, Z) * BLOCK + half * HALF, HALF), HALF)

    sends = []

    def zsend(c, slot, src, dst, device):
        copy = remote(src, dst, zs_sem.at[c, slot], zr_sem.at[c, slot], device)
        copy.start()
        sends.append(copy)

    def zwait(c, slot, dst):
        remote(dst, dst, zs_sem.at[c, slot], zr_sem.at[c, slot], plus).wait_recv()

    def first(c):
        relayed(0, wr, c)

        @pl.loop(0, WIDTH // 32)
        def _(i):
            rows = pl.ds(pl.multiple_of(i * 32, 32), 32)
            pair = jnp.swapaxes(wr[c, rows], 0, 1)
            wd[c, rows, 0:FC] = pair[0]
            wd[c, rows, FC : 2 * FC] = pair[1]

        @pl.loop(0, 4)
        def _(slot):
            late = lax.div(slot, 2)
            odd = lax.rem(slot, 2)
            step = 2 + late * (2 * odd - 1)
            half = odd + late * (1 - 2 * odd)
            sb[c, slot] = dot(a[tokens(step, half), :], wd[c]).astype(BF16)

        zsend(c, 0, sb.at[c, 0], rmid.at[c, 0], plus)
        zsend(c, 1, sb.at[c, 1], rmid.at[c, 1], minus)
        zsend(c, 2, sb.at[c, 2], rfin.at[c, 0, 1], plus)
        zsend(c, 3, sb.at[c, 3], rfin.at[c, 1, 0], minus)

    def second(c):
        zwait(c, 0, rmid.at[c, 0])
        zwait(c, 1, rmid.at[c, 1])

        @pl.loop(0, 2)
        def _(slot):
            sb[c, 4 + slot] = (
                dot(a[tokens(1 + 2 * slot, slot), :], wd[c]) + rmid[c, slot].astype(F32)
            ).astype(BF16)

        zsend(c, 4, sb.at[c, 4], rfin.at[c, 0, 0], plus)
        zsend(c, 5, sb.at[c, 5], rfin.at[c, 1, 1], minus)

    def block_sum(c, half):
        return (
            dot(a[tokens(0, half), :], wd[c])
            + rfin[c, 0, half].astype(F32)
            + rfin[c, 1, half].astype(F32)
        )

    def third(c):
        zwait(c, 2, rfin.at[c, 0, 1])
        zwait(c, 3, rfin.at[c, 1, 0])
        zwait(c, 4, rfin.at[c, 0, 0])
        zwait(c, 5, rfin.at[c, 1, 1])
        yls[c] = block_sum(c, 1 - lo).astype(BF16)
        zsend(c, 6, yls.at[c], ylr.at[c], mate)

    def fourth(c):
        zwait(c, 6, ylr.at[c])
        sums = (block_sum(c, lo) + ylr[c].astype(F32)) * width_scale
        gate, up = sums[:, :FC], sums[:, FC:]
        span = slice(c * FC, (c + 1) * FC)
        activated, slope = gelu_parts(gate)
        upstream = cot[:, span].astype(F32)
        hid[:, span] = (activated * up).astype(BF16)
        rows = tokens(0, lo)
        grads[c, rows, 0:FC] = (upstream * up * slope).astype(BF16)
        grads[c, rows, FC : 2 * FC] = (upstream * activated).astype(BF16)
        mine = grads.at[c, rows]
        zsend(c, 7, mine, mine, mate)

    def fifth(c):
        mine = grads.at[c, tokens(0, lo)]
        zsend(c, 8, mine, mine, plus)
        zsend(c, 9, mine, mine, minus)
        theirs = grads.at[c, tokens(0, 1 - lo)]
        zwait(c, 7, theirs)
        zsend(c, 10, theirs, theirs, plus)
        zsend(c, 11, theirs, theirs, minus)

    def sixth(c):
        below, above = grads.at[c, tokens(3, lo)], grads.at[c, tokens(1, 1 - lo)]
        zwait(c, 8, below)
        zsend(c, 12, below, below, plus)
        zwait(c, 11, above)
        zsend(c, 13, above, above, minus)

    def gathered(c):
        zwait(c, 9, grads.at[c, tokens(1, lo)])
        zwait(c, 10, grads.at[c, tokens(3, 1 - lo)])
        zwait(c, 12, grads.at[c, tokens(2, lo)])
        zwait(c, 13, grads.at[c, tokens(2, 1 - lo)])

    def back(c):
        @pl.loop(0, TOK // HALF)
        def _(i):
            rows = pl.ds(pl.multiple_of(i * HALF, HALF), HALF)
            term = lax.dot_general(
                grads[c, rows, :], wd[c], (((1,), (1,)), ((), ())), preferred_element_type=F32
            )
            if c == 0:
                acc[rows, :] = term
            else:
                acc[rows, :] += term

    outs = ((nws, nw), (nms, nm), (nvs, nv))

    def written(c):
        span = pl.ds(c * FC, FC)
        return [
            pltpu.make_async_copy(held, out.at[:, :, span], out_sem.at[i]) for i, (held, out) in enumerate(outs)
        ]

    def weight_grads(c):
        @pl.loop(0, 3)
        def _(i):
            rows = pl.ds(pl.multiple_of(i * 192, 192), 192)
            both = dot(at[rows, :], grads[c]) * width_scale
            gw[0, rows, :] = both[:, :FC]
            gw[1, rows, :] = both[:, FC:]

    def update(c):
        relayed(1, mr, c)
        relayed(2, vr, c)
        if c > 0:
            for copy in written(c - 1):
                copy.wait()

        @pl.loop(0, WIDTH // 32)
        def _(i):
            rows = pl.ds(pl.multiple_of(i * 32, 32), 32)
            mean = jnp.swapaxes(mr[c, rows], 0, 1)
            var = jnp.swapaxes(vr[c, rows], 0, 1)
            for k in range(2):
                grad = gw[k, rows, :]
                moment_one = beta_one * mean[k].astype(F32) + (1.0 - beta_one) * grad
                var_next = beta_two * var[k].astype(F32) + (1.0 - beta_two) * grad * grad
                mean_hat = moment_one * (1.0 / (1.0 - beta_one**RESUME_STEP))
                var_hat = var_next * (1.0 / (1.0 - beta_two**RESUME_STEP))
                master = wd[c, rows, k * FC : (k + 1) * FC].astype(F32)
                updated = master * (1.0 - learn_rate * decay_rate) - learn_rate * mean_hat / (
                    jnp.sqrt(var_hat) + epsilon
                )
                nws[k, rows, :] = updated.astype(BF16)
                nms[k, rows, :] = moment_one.astype(BF16)
                nvs[k, rows, :] = var_next

        for copy in written(c):
            copy.start()

    def stages(step):
        def at_lag(lag):
            return 0 <= step - lag < CH

        if at_lag(0):
            first(step)
        if at_lag(1):
            second(step - 1)
        if step + 2 < CH:
            relay(0, w_in, wr, step + 2)
        if at_lag(2):
            third(step - 2)
        if at_lag(3):
            fourth(step - 3)
            relay(1, m_in, mr, step - 3)
        if at_lag(4):
            relay(2, vb, vr, step - 4)
        if at_lag(LAG):
            fifth(step - LAG)
        if at_lag(LAG + 1):
            sixth(step - LAG - 1)
        if at_lag(LAG + 2) and step - LAG - 2 < CH - 1:
            gathered(step - LAG - 2)
            back(step - LAG - 2)
            weight_grads(step - LAG - 2)
            update(step - LAG - 2)

    for step in range(CH + LAG + 2):
        stages(step)

    gathered(CH - 1)

    def swap(j):
        return remote(xs.at[j], xr.at[j], x_send.at[j], x_recv.at[j], twin)

    def acc_rows(index):
        return pl.ds(pl.multiple_of(index * OWN, OWN), OWN)

    @pl.loop(1, 9)
    def _(i):
        j = peer_line(lax.rem(i, 8))
        rows = pl.ds(pl.multiple_of(j * HALF, HALF), HALF)
        acc[rows, :] += lax.dot_general(
            grads[CH - 1, rows, :], wd[CH - 1], (((1,), (1,)), ((), ())), preferred_element_type=F32
        )
        xs[j] = acc[acc_rows(j * 2 + 1 - core), :].astype(BF16)
        swap(j).start()

    @pl.loop(1, 9)
    def _(i):
        j = peer_line(lax.rem(i, 8))
        swap(j).wait_recv()
        rows = acc_rows(j * 2 + core)
        total = acc[rows, :] + xr[j].astype(F32)
        acc[rows, :] = total

        @pl.when(i < 8)
        def _():
            xq[i - 1] = total.astype(BF16)
            remote(xq.at[i - 1], xf.at[i - 1], p_send, p_recv, (j * 2 + core, mp)).start()

    weight_grads(CH - 1)
    update(CH - 1)
    pltpu.make_async_copy(xf, xf, p_recv).wait()
    total = acc[acc_rows(dp), :]
    for i in range(7):
        total = total + xf[i].astype(F32)
    ig[...] = (total * width_scale).T.astype(BF16)

    pltpu.make_async_copy(xf, xf, p_send).wait()

    @pl.loop(0, 8)
    def _(j):
        swap(j).wait_send()

    for copy in written(CH - 1):
        copy.wait()
    for copy in sends:
        copy.wait_send()
    for c in range(CH):
        relay_sent(0, wr, c)
        relay_sent(1, mr, c)
        relay_sent(2, vr, c)
    seven = at.at[:, pl.ds(0, 7 * OWN)]
    pltpu.make_async_copy(seven, seven, act_send).wait()
    pltpu.make_async_copy(half_acts, half_acts, fwd_send).wait()


def shards(acts, old_weights, old_mean, old_var, cotangent):
    vmem = pl.BlockSpec(memory_space=pltpu.VMEM)
    hbm = pl.BlockSpec(memory_space=pl.ANY)
    dma = pltpu.SemaphoreType.DMA
    macs = 3 * TOK * WIDTH * 2 * FS

    hidden, input_grad, new_weights, new_mean, new_var = pl.pallas_call(
        kernel,
        out_shape=(
            jax.ShapeDtypeStruct((HALF, FS), BF16),
            jax.ShapeDtypeStruct((WIDTH, OWN), BF16),
            jax.ShapeDtypeStruct((2, WIDTH, FS), BF16),
            jax.ShapeDtypeStruct((2, WIDTH, FS), BF16),
            jax.ShapeDtypeStruct((2, WIDTH, FS), F32),
        ),
        in_specs=[hbm, hbm, hbm, hbm, vmem],
        out_specs=(vmem, vmem, hbm, hbm, hbm),
        scratch_shapes=[
            pltpu.VMEM((2, PIECE, 2, FS * DP), F32),
            pltpu.VMEM((ROWS, 2, FS * DP), BF16),
            pltpu.VMEM((WIDTH, TOK), BF16),
            pltpu.VMEM((TOK, WIDTH), BF16),
            pltpu.VMEM((CH, WIDTH, 2, FC), BF16),
            pltpu.VMEM((CH, WIDTH, 2, FC), BF16),
            pltpu.VMEM((CH, WIDTH, 2, FC), BF16),
            pltpu.VMEM((CH, WIDTH, 2 * FC), BF16),
            pltpu.VMEM((CH, 6, HALF, 2 * FC), BF16),
            pltpu.VMEM((CH, 2, HALF, 2 * FC), BF16),
            pltpu.VMEM((CH, 2, 2, HALF, 2 * FC), BF16),
            pltpu.VMEM((CH, HALF, 2 * FC), BF16),
            pltpu.VMEM((CH, HALF, 2 * FC), BF16),
            pltpu.VMEM((CH, TOK, 2 * FC), BF16),
            pltpu.VMEM((TOK, WIDTH), F32),
            pltpu.VMEM((2, WIDTH, FC), F32),
            pltpu.VMEM((2, WIDTH, FC), BF16),
            pltpu.VMEM((2, WIDTH, FC), BF16),
            pltpu.VMEM((2, WIDTH, FC), F32),
            pltpu.VMEM((8, OWN, WIDTH), BF16),
            pltpu.VMEM((8, OWN, WIDTH), BF16),
            pltpu.VMEM((7, OWN, WIDTH), BF16),
            pltpu.VMEM((7, OWN, WIDTH), BF16),
            dma, dma((2,)), dma((3,)), dma, dma((7,)), dma, dma, dma((3, CH)), dma((3, CH)),
            dma((CH, 14)), dma((CH, 14)), dma((8,)), dma((8,)), dma, dma,
        ],
        compiler_params=pltpu.CompilerParams(
            collective_id=0, has_side_effects=True, vmem_limit_bytes=63 * 2**20
        ),
        cost_estimate=pl.CostEstimate(flops=2 * macs, bytes_accessed=40 * 2**20, transcendentals=0),
    )(
        acts.T,
        jnp.transpose(old_weights, (1, 0, 2)),
        jnp.transpose(old_mean, (1, 0, 2)),
        jnp.transpose(old_var, (1, 0, 2)),
        cotangent,
    )
    return hidden, input_grad.T, new_weights, new_mean, new_var


def solution(mesh):
    placed = (
        P("dp", "mp"),
        P(None, ("mp", "dp"), None),
        P(None, ("mp", "dp"), None),
        P(None, ("mp", "dp"), None),
        P("mp", "dp"),
    )
    return jax.shard_map(
        shards,
        mesh=mesh,
        in_specs=placed,
        out_specs=(
            P("mp", "dp"),
            P("dp", "mp"),
            P(None, "mp", "dp"),
            P(None, "mp", "dp"),
            P(None, "mp", "dp"),
        ),
        check_vma=False,
    )
```

```python
import functools

import jax
import jax.numpy as jnp
from jax import lax
from jax.experimental import pallas as pl
from jax.experimental.pallas import tpu as pltpu
from jax.sharding import PartitionSpec as P

D = 4608
RESUME_STEP = 1000

tanh_coef = 0.7978845608028654
cube_coef = 0.044715
beta_one = 0.9
beta_two = 0.95
learn_rate = 0.05
decay_rate = 0.1
epsilon = 1e-08
width_scale = D ** (-0.5)

MESH = pl.DeviceIdType.MESH
F32 = jnp.float32
BF16 = jnp.bfloat16

DP, Z, LO = 16, 4, 2
ROWS = 36
WIDTH = ROWS * DP
TOK = 2048
BLOCK = TOK // Z
HALF = BLOCK // LO
FS = 1152
CH = 9
FC = FS // CH
AHEAD = 4
LATE = 2
LAG = 4
PIECE = 9
OWN = TOK // DP


def gelu_parts(value):
    inner = jnp.tanh(tanh_coef * (value + cube_coef * value * value * value))
    activated = 0.5 * value * (1.0 + inner)
    slope = 0.5 * (1.0 + inner) + 0.5 * value * (1.0 - inner * inner) * tanh_coef * (
        1.0 + 3.0 * cube_coef * value * value
    )
    return activated, slope


def dot(left, right):
    return jnp.dot(left, right, preferred_element_type=F32)


def kernel(
    at_in, w_in, m_in, v_in, cot, hid, ig, nw, nm, nv,
    vf, vb, at, a, wr, mr, vr, wd, sb, rmid, rfin, yls, ylr, grads, acc, gw, nws, nms, nvs, xs, xr, xq, xf,
    copy_sem, cast_sem, out_sem, act_send, act_recv, fwd_send, fwd_recv, rel_send, rel_recv,
    zs_sem, zr_sem, x_send, x_recv, p_send, p_recv,
):
    dp, mp = lax.axis_index("dp"), lax.axis_index("mp")
    core = lax.rem(dp, 2)
    line = lax.div(dp, 2)
    x = lax.rem(line, 4)
    y_hi = lax.div(line, 4)
    z = lax.div(mp, 2)
    lo = lax.rem(mp, 2)

    def z_dev(step):
        return (dp, lax.rem(z + step, Z) * 2 + lo)

    plus, minus = z_dev(1), z_dev(Z - 1)
    mate = (dp, z * 2 + 1 - lo)
    twin = (dp + 1 - 2 * core, mp)

    def peer_dp(i):
        far = 1 - lax.rem(i, 2)
        j = lax.div(i, 2) + lax.rem(i, 2)
        q = lax.div(j, 2)
        step = q + lax.div(q, 2) * (1 - 2 * lax.rem(q, 2))
        other = lax.rem(core + lax.rem(j, 2), 2)
        return lax.rem(y_hi + far, 2) * 8 + lax.rem(x + step, 4) * 2 + other

    def peer_line(i):
        far = lax.rem(i, 2)
        q = lax.div(i, 2)
        step = q + lax.div(q, 2) * (1 - 2 * lax.rem(q, 2))
        return lax.rem(y_hi + far, 2) * 4 + lax.rem(x + step, 4)

    def cast_part(i):
        return pltpu.make_async_copy(v_in.at[pl.ds(i * PIECE, PIECE)], vf.at[i % 2], cast_sem.at[i % 2])

    cast_part(0).start()
    cast_part(1).start()

    barrier = pltpu.get_barrier_semaphore()

    @pl.loop(0, DP - 1)
    def _(i):
        pl.semaphore_signal(barrier, inc=1, device_id=(peer_dp(i), mp), device_id_type=MESH)

    for other in (plus, minus, mate):
        pl.semaphore_signal(barrier, inc=1, device_id=other, device_id_type=MESH)
    pl.semaphore_wait(barrier, DP - 1 + 3)

    def remote(src, dst, send, recv, device):
        return pltpu.make_async_remote_copy(
            src_ref=src, dst_ref=dst, send_sem=send, recv_sem=recv, device_id=device, device_id_type=MESH
        )

    def cols(index):
        return pl.ds(pl.multiple_of(index * OWN, OWN), OWN)

    own_act = pltpu.make_async_copy(at_in, at.at[:, cols(dp)], copy_sem)
    own_act.start()

    @pl.loop(1, 8)
    def _(i):
        remote(at_in, at.at[:, cols(dp)], act_send, act_recv.at[i - 1], (peer_line(i) * 2 + core, mp)).start()

    remote(at_in, at.at[:, cols(dp)], fwd_send, fwd_recv.at[line], twin).start()

    def relay(index, src, dst, c):
        mine = pl.ds(dp * ROWS, ROWS)

        def part(owner):
            return src.at[:, :, pl.ds(pl.multiple_of(owner * FS + c * FC, 128), FC)]

        pltpu.make_async_copy(part(dp), dst.at[c, mine], rel_recv.at[index, c]).start()

        @pl.loop(0, DP - 1)
        def _(i):
            owner = peer_dp(i)
            remote(part(owner), dst.at[c, mine], rel_send.at[index, c], rel_recv.at[index, c], (owner, mp)).start()

    def relayed(index, dst, c):
        pltpu.make_async_copy(dst.at[c], dst.at[c], rel_recv.at[index, c]).wait()

    def relay_sent(index, dst, c):
        sent = dst.at[c, pl.ds(0, WIDTH - ROWS)]
        pltpu.make_async_copy(sent, sent, rel_send.at[index, c]).wait()

    for c in range(AHEAD):
        relay(0, w_in, wr, c)

    for i in range(ROWS // PIECE):
        cast_part(i).wait()

        @pl.loop(0, PIECE)
        def _(row):
            vb[i * PIECE + row] = vf[i % 2, row].astype(BF16)

        if i + 2 < ROWS // PIECE:
            cast_part(i + 2).start()

    def turn(index):
        a[pl.ds(pl.multiple_of(index * OWN, OWN), OWN), :] = at[:, cols(index)].T

    own_act.wait()
    turn(dp)

    @pl.loop(1, 8)
    def _(i):
        far = lax.rem(i, 2)
        q = lax.div(i, 2)
        step = q + lax.div(q, 2) * (1 - 2 * lax.rem(q, 2))
        source = (lax.rem(y_hi + far, 2) * 4 + lax.rem(x + 4 - step, 4)) * 2 + core
        block = at.at[:, cols(source)]
        remote(block, block, act_send, act_recv.at[i - 1], twin).wait_recv()
        remote(block, block, fwd_send, fwd_recv.at[lax.div(source, 2)], twin).start()
        turn(source)

    half_acts = at.at[:, pl.ds(0, TOK // 2)]

    @pl.loop(0, DP // 2)
    def _(i):
        far = lax.rem(i, 2)
        q = lax.div(i, 2)
        step = q + lax.div(q, 2) * (1 - 2 * lax.rem(q, 2))
        origin = lax.rem(y_hi + far, 2) * 4 + lax.rem(x + 4 - step, 4)
        block = at.at[:, cols(origin * 2 + 1 - core)]
        remote(block, block, fwd_send, fwd_recv.at[origin], twin).wait_recv()
        turn(origin * 2 + 1 - core)

    def tokens(step, half):
        return pl.ds(pl.multiple_of(lax.rem(z + step, Z) * BLOCK + half * HALF, HALF), HALF)

    sends = []

    def zsend(c, slot, src, dst, device):
        copy = remote(src, dst, zs_sem.at[c, slot], zr_sem.at[c, slot], device)
        copy.start()
        sends.append(copy)

    def zwait(c, slot, dst):
        remote(dst, dst, zs_sem.at[c, slot], zr_sem.at[c, slot], plus).wait_recv()

    def first(c):
        relayed(0, wr, c)

        @pl.loop(0, WIDTH // 32)
        def _(i):
            rows = pl.ds(pl.multiple_of(i * 32, 32), 32)
            pair = jnp.swapaxes(wr[c, rows], 0, 1)
            wd[c, rows, 0:FC] = pair[0]
            wd[c, rows, FC : 2 * FC] = pair[1]

        @pl.loop(0, 2)
        def _(slot):
            sb[c, slot] = dot(a[tokens(2, slot), :], wd[c]).astype(BF16)

        zsend(c, 0, sb.at[c, 0], rmid.at[c, 0], plus)
        zsend(c, 1, sb.at[c, 1], rmid.at[c, 1], minus)

        @pl.loop(0, 2)
        def _(slot):
            sb[c, 2 + slot] = dot(a[tokens(1 + 2 * slot, 1 - slot), :], wd[c]).astype(BF16)

        zsend(c, 2, sb.at[c, 2], rfin.at[c, 0, 1], plus)
        zsend(c, 3, sb.at[c, 3], rfin.at[c, 1, 0], minus)

    def second(c):
        zwait(c, 0, rmid.at[c, 0])
        zwait(c, 1, rmid.at[c, 1])

        @pl.loop(0, 2)
        def _(slot):
            sb[c, 4 + slot] = (
                dot(a[tokens(1 + 2 * slot, slot), :], wd[c]) + rmid[c, slot].astype(F32)
            ).astype(BF16)

        zsend(c, 4, sb.at[c, 4], rfin.at[c, 0, 0], plus)
        zsend(c, 5, sb.at[c, 5], rfin.at[c, 1, 1], minus)

    def block_sum(c, half):
        return (
            dot(a[tokens(0, half), :], wd[c])
            + rfin[c, 0, half].astype(F32)
            + rfin[c, 1, half].astype(F32)
        )

    def third(c):
        zwait(c, 2, rfin.at[c, 0, 1])
        zwait(c, 3, rfin.at[c, 1, 0])
        zwait(c, 4, rfin.at[c, 0, 0])
        zwait(c, 5, rfin.at[c, 1, 1])
        yls[c] = block_sum(c, 1 - lo).astype(BF16)
        zsend(c, 6, yls.at[c], ylr.at[c], mate)

    def fourth(c):
        zwait(c, 6, ylr.at[c])
        sums = (block_sum(c, lo) + ylr[c].astype(F32)) * width_scale
        gate, up = sums[:, :FC], sums[:, FC:]
        span = slice(c * FC, (c + 1) * FC)
        activated, slope = gelu_parts(gate)
        upstream = cot[:, span].astype(F32)
        hid[:, span] = (activated * up).astype(BF16)
        rows = tokens(0, lo)
        grads[c, rows, 0:FC] = (upstream * up * slope).astype(BF16)
        grads[c, rows, FC : 2 * FC] = (upstream * activated).astype(BF16)
        mine = grads.at[c, rows]
        zsend(c, 7, mine, mine, mate)

    def fifth(c):
        mine = grads.at[c, tokens(0, lo)]
        zsend(c, 8, mine, mine, plus)
        zsend(c, 9, mine, mine, minus)
        theirs = grads.at[c, tokens(0, 1 - lo)]
        zwait(c, 7, theirs)
        zsend(c, 10, theirs, theirs, plus)
        zsend(c, 11, theirs, theirs, minus)

    def sixth(c):
        below, above = grads.at[c, tokens(3, lo)], grads.at[c, tokens(1, 1 - lo)]
        zwait(c, 8, below)
        zsend(c, 12, below, below, plus)
        zwait(c, 11, above)
        zsend(c, 13, above, above, minus)

    def gathered(c):
        zwait(c, 9, grads.at[c, tokens(1, lo)])
        zwait(c, 10, grads.at[c, tokens(3, 1 - lo)])
        zwait(c, 12, grads.at[c, tokens(2, lo)])
        zwait(c, 13, grads.at[c, tokens(2, 1 - lo)])

    def back(c):
        @pl.loop(0, TOK // HALF)
        def _(i):
            rows = pl.ds(pl.multiple_of(i * HALF, HALF), HALF)
            term = lax.dot_general(
                grads[c, rows, :], wd[c], (((1,), (1,)), ((), ())), preferred_element_type=F32
            )
            if c == 0:
                acc[rows, :] = term
            else:
                acc[rows, :] += term

    outs = ((nws, nw), (nms, nm), (nvs, nv))

    def written(c):
        span = pl.ds(c * FC, FC)
        return [
            pltpu.make_async_copy(held, out.at[:, :, span], out_sem.at[i]) for i, (held, out) in enumerate(outs)
        ]

    def weight_grads(c):
        @pl.loop(0, 3)
        def _(i):
            rows = pl.ds(pl.multiple_of(i * 192, 192), 192)
            both = dot(at[rows, :], grads[c]) * width_scale
            gw[0, rows, :] = both[:, :FC]
            gw[1, rows, :] = both[:, FC:]

    def update(c):
        relayed(1, mr, c)
        relayed(2, vr, c)
        if c > 0:
            for copy in written(c - 1):
                copy.wait()

        @pl.loop(0, WIDTH // 32)
        def _(i):
            rows = pl.ds(pl.multiple_of(i * 32, 32), 32)
            mean = jnp.swapaxes(mr[c, rows], 0, 1)
            var = jnp.swapaxes(vr[c, rows], 0, 1)
            for k in range(2):
                grad = gw[k, rows, :]
                moment_one = beta_one * mean[k].astype(F32) + (1.0 - beta_one) * grad
                var_next = beta_two * var[k].astype(F32) + (1.0 - beta_two) * grad * grad
                mean_hat = moment_one * (1.0 / (1.0 - beta_one**RESUME_STEP))
                var_hat = var_next * (1.0 / (1.0 - beta_two**RESUME_STEP))
                master = wd[c, rows, k * FC : (k + 1) * FC].astype(F32)
                updated = master * (1.0 - learn_rate * decay_rate) - learn_rate * mean_hat / (
                    jnp.sqrt(var_hat) + epsilon
                )
                nws[k, rows, :] = updated.astype(BF16)
                nms[k, rows, :] = moment_one.astype(BF16)
                nvs[k, rows, :] = var_next

        for copy in written(c):
            copy.start()

    def stages(step):
        def at_lag(lag):
            return 0 <= step - lag < CH

        if at_lag(0):
            first(step)
        if at_lag(1):
            second(step - 1)
        if step + AHEAD < CH:
            relay(0, w_in, wr, step + AHEAD)
        if at_lag(2):
            third(step - 2)
        if at_lag(3):
            fourth(step - 3)
            relay(1, m_in, mr, step - 3)
        if at_lag(4):
            relay(2, vb, vr, step - 4)
        if at_lag(LAG):
            fifth(step - LAG)
        if at_lag(LAG + 1):
            sixth(step - LAG - 1)
        if at_lag(LAG + 2) and step - LAG - 2 < CH - 1:
            gathered(step - LAG - 2)
            back(step - LAG - 2)
            if step - LAG - 2 < CH - LATE:
                weight_grads(step - LAG - 2)
                update(step - LAG - 2)

    for step in range(CH + LAG + 2):
        stages(step)

    gathered(CH - 1)

    def swap(j):
        return remote(xs.at[j], xr.at[j], x_send.at[j], x_recv.at[j], twin)

    def acc_rows(index):
        return pl.ds(pl.multiple_of(index * OWN, OWN), OWN)

    @pl.loop(1, 9)
    def _(i):
        j = peer_line(lax.rem(i, 8))
        rows = pl.ds(pl.multiple_of(j * HALF, HALF), HALF)
        acc[rows, :] += lax.dot_general(
            grads[CH - 1, rows, :], wd[CH - 1], (((1,), (1,)), ((), ())), preferred_element_type=F32
        )
        xs[j] = acc[acc_rows(j * 2 + 1 - core), :].astype(BF16)
        swap(j).start()

    @pl.loop(1, 9)
    def _(i):
        j = peer_line(lax.rem(i, 8))
        swap(j).wait_recv()
        rows = acc_rows(j * 2 + core)
        total = acc[rows, :] + xr[j].astype(F32)
        acc[rows, :] = total

        @pl.when(i < 8)
        def _():
            xq[i - 1] = total.astype(BF16)
            remote(xq.at[i - 1], xf.at[i - 1], p_send, p_recv, (j * 2 + core, mp)).start()

    for c in range(CH - LATE, CH):
        weight_grads(c)
        update(c)

    pltpu.make_async_copy(xf, xf, p_recv).wait()
    total = acc[acc_rows(dp), :]
    for i in range(7):
        total = total + xf[i].astype(F32)
    ig[...] = (total * width_scale).T.astype(BF16)

    pltpu.make_async_copy(xf, xf, p_send).wait()

    @pl.loop(0, 8)
    def _(j):
        swap(j).wait_send()

    for copy in written(CH - 1):
        copy.wait()
    for copy in sends:
        copy.wait_send()
    for c in range(CH):
        relay_sent(0, wr, c)
        relay_sent(1, mr, c)
        relay_sent(2, vr, c)
    seven = at.at[:, pl.ds(0, 7 * OWN)]
    pltpu.make_async_copy(seven, seven, act_send).wait()
    pltpu.make_async_copy(half_acts, half_acts, fwd_send).wait()


def shards(acts, old_weights, old_mean, old_var, cotangent):
    vmem = pl.BlockSpec(memory_space=pltpu.VMEM)
    hbm = pl.BlockSpec(memory_space=pl.ANY)
    dma = pltpu.SemaphoreType.DMA
    macs = 3 * TOK * WIDTH * 2 * FS

    hidden, input_grad, new_weights, new_mean, new_var = pl.pallas_call(
        kernel,
        out_shape=(
            jax.ShapeDtypeStruct((HALF, FS), BF16),
            jax.ShapeDtypeStruct((WIDTH, OWN), BF16),
            jax.ShapeDtypeStruct((2, WIDTH, FS), BF16),
            jax.ShapeDtypeStruct((2, WIDTH, FS), BF16),
            jax.ShapeDtypeStruct((2, WIDTH, FS), F32),
        ),
        in_specs=[hbm, hbm, hbm, hbm, vmem],
        out_specs=(vmem, vmem, hbm, hbm, hbm),
        scratch_shapes=[
            pltpu.VMEM((2, PIECE, 2, FS * DP), F32),
            pltpu.VMEM((ROWS, 2, FS * DP), BF16),
            pltpu.VMEM((WIDTH, TOK), BF16),
            pltpu.VMEM((TOK, WIDTH), BF16),
            pltpu.VMEM((CH, WIDTH, 2, FC), BF16),
            pltpu.VMEM((CH, WIDTH, 2, FC), BF16),
            pltpu.VMEM((CH, WIDTH, 2, FC), BF16),
            pltpu.VMEM((CH, WIDTH, 2 * FC), BF16),
            pltpu.VMEM((CH, 6, HALF, 2 * FC), BF16),
            pltpu.VMEM((CH, 2, HALF, 2 * FC), BF16),
            pltpu.VMEM((CH, 2, 2, HALF, 2 * FC), BF16),
            pltpu.VMEM((CH, HALF, 2 * FC), BF16),
            pltpu.VMEM((CH, HALF, 2 * FC), BF16),
            pltpu.VMEM((CH, TOK, 2 * FC), BF16),
            pltpu.VMEM((TOK, WIDTH), F32),
            pltpu.VMEM((2, WIDTH, FC), F32),
            pltpu.VMEM((2, WIDTH, FC), BF16),
            pltpu.VMEM((2, WIDTH, FC), BF16),
            pltpu.VMEM((2, WIDTH, FC), F32),
            pltpu.VMEM((8, OWN, WIDTH), BF16),
            pltpu.VMEM((8, OWN, WIDTH), BF16),
            pltpu.VMEM((7, OWN, WIDTH), BF16),
            pltpu.VMEM((7, OWN, WIDTH), BF16),
            dma, dma((2,)), dma((3,)), dma, dma((7,)), dma, dma((DP // 2,)), dma((3, CH)), dma((3, CH)),
            dma((CH, 14)), dma((CH, 14)), dma((8,)), dma((8,)), dma, dma,
        ],
        compiler_params=pltpu.CompilerParams(
            collective_id=0, has_side_effects=True, vmem_limit_bytes=63 * 2**20
        ),
        cost_estimate=pl.CostEstimate(flops=2 * macs, bytes_accessed=40 * 2**20, transcendentals=0),
    )(
        acts.T,
        jnp.transpose(old_weights, (1, 0, 2)),
        jnp.transpose(old_mean, (1, 0, 2)),
        jnp.transpose(old_var, (1, 0, 2)),
        cotangent,
    )
    return hidden, input_grad.T, new_weights, new_mean, new_var


def solution(mesh):
    placed = (
        P("dp", "mp"),
        P(None, ("mp", "dp"), None),
        P(None, ("mp", "dp"), None),
        P(None, ("mp", "dp"), None),
        P("mp", "dp"),
    )
    return jax.shard_map(
        shards,
        mesh=mesh,
        in_specs=placed,
        out_specs=(
            P("mp", "dp"),
            P("dp", "mp"),
            P(None, "mp", "dp"),
            P(None, "mp", "dp"),
            P(None, "mp", "dp"),
        ),
        check_vma=False,
    )
```

```python
import functools

import jax
import jax.numpy as jnp
from jax import lax
from jax.experimental import pallas as pl
from jax.experimental.pallas import tpu as pltpu
from jax.sharding import PartitionSpec as P

D = 4608
RESUME_STEP = 1000

tanh_coef = 0.7978845608028654
cube_coef = 0.044715
beta_one = 0.9
beta_two = 0.95
learn_rate = 0.05
decay_rate = 0.1
epsilon = 1e-08
width_scale = D ** (-0.5)

MESH = pl.DeviceIdType.MESH
F32 = jnp.float32
BF16 = jnp.bfloat16

DP, Z, LO = 16, 4, 2
ROWS = 36
WIDTH = ROWS * DP
TOK = 2048
BLOCK = TOK // Z
HALF = BLOCK // LO
FS = 1152
CH = 9
FC = FS // CH
AHEAD = 4
LATE = 2
LAG = 4
PIECE = 9
OWN = TOK // DP


def gelu_parts(value):
    inner = jnp.tanh(tanh_coef * (value + cube_coef * value * value * value))
    activated = 0.5 * value * (1.0 + inner)
    slope = 0.5 * (1.0 + inner) + 0.5 * value * (1.0 - inner * inner) * tanh_coef * (
        1.0 + 3.0 * cube_coef * value * value
    )
    return activated, slope


def dot(left, right):
    return jnp.dot(left, right, preferred_element_type=F32)


def kernel(
    at_in, w_in, m_in, v_in, cot, hid, ig, nw, nm, nv,
    vf, vb, at, a, wr, mr, vr, wd, sb, rmid, rfin, yls, ylr, grads, acc, gw, nws, nms, nvs, xr, xq, xf,
    copy_sem, cast_sem, out_sem, act_send, act_recv, fwd_send, fwd_recv, rel_send, rel_recv,
    zs_sem, zr_sem, x_send, x_recv, p_send, p_recv,
):
    dp, mp = lax.axis_index("dp"), lax.axis_index("mp")
    core = lax.rem(dp, 2)
    line = lax.div(dp, 2)
    x = lax.rem(line, 4)
    y_hi = lax.div(line, 4)
    z = lax.div(mp, 2)
    lo = lax.rem(mp, 2)

    def z_dev(step):
        return (dp, lax.rem(z + step, Z) * 2 + lo)

    plus, minus = z_dev(1), z_dev(Z - 1)
    mate = (dp, z * 2 + 1 - lo)
    twin = (dp + 1 - 2 * core, mp)

    def peer_dp(i):
        far = 1 - lax.rem(i, 2)
        j = lax.div(i, 2) + lax.rem(i, 2)
        q = lax.div(j, 2)
        step = q + lax.div(q, 2) * (1 - 2 * lax.rem(q, 2))
        other = lax.rem(core + lax.rem(j, 2), 2)
        return lax.rem(y_hi + far, 2) * 8 + lax.rem(x + step, 4) * 2 + other

    def peer_line(i):
        far = lax.rem(i, 2)
        q = lax.div(i, 2)
        step = q + lax.div(q, 2) * (1 - 2 * lax.rem(q, 2))
        return lax.rem(y_hi + far, 2) * 4 + lax.rem(x + step, 4)

    def cast_part(i):
        return pltpu.make_async_copy(v_in.at[pl.ds(i * PIECE, PIECE)], vf.at[i % 2], cast_sem.at[i % 2])

    cast_part(0).start()
    cast_part(1).start()

    barrier = pltpu.get_barrier_semaphore()

    @pl.loop(0, DP - 1)
    def _(i):
        pl.semaphore_signal(barrier, inc=1, device_id=(peer_dp(i), mp), device_id_type=MESH)

    for other in (plus, minus, mate):
        pl.semaphore_signal(barrier, inc=1, device_id=other, device_id_type=MESH)
    pl.semaphore_wait(barrier, DP - 1 + 3)

    def remote(src, dst, send, recv, device):
        return pltpu.make_async_remote_copy(
            src_ref=src, dst_ref=dst, send_sem=send, recv_sem=recv, device_id=device, device_id_type=MESH
        )

    def cols(index):
        return pl.ds(pl.multiple_of(index * OWN, OWN), OWN)

    own_act = pltpu.make_async_copy(at_in, at.at[:, cols(dp)], copy_sem)
    own_act.start()

    @pl.loop(1, 8)
    def _(i):
        remote(at_in, at.at[:, cols(dp)], act_send, act_recv.at[i - 1], (peer_line(i) * 2 + core, mp)).start()

    remote(at_in, at.at[:, cols(dp)], fwd_send, fwd_recv.at[line], twin).start()

    def relay(index, src, dst, c):
        mine = pl.ds(dp * ROWS, ROWS)

        def part(owner):
            return src.at[:, :, pl.ds(pl.multiple_of(owner * FS + c * FC, 128), FC)]

        pltpu.make_async_copy(part(dp), dst.at[c, mine], rel_recv.at[index, c]).start()

        @pl.loop(0, DP - 1)
        def _(i):
            owner = peer_dp(i)
            remote(part(owner), dst.at[c, mine], rel_send.at[index, c], rel_recv.at[index, c], (owner, mp)).start()

    def relayed(index, dst, c):
        pltpu.make_async_copy(dst.at[c], dst.at[c], rel_recv.at[index, c]).wait()

    def relay_sent(index, dst, c):
        sent = dst.at[c, pl.ds(0, WIDTH - ROWS)]
        pltpu.make_async_copy(sent, sent, rel_send.at[index, c]).wait()

    for c in range(AHEAD):
        relay(0, w_in, wr, c)

    for i in range(ROWS // PIECE):
        cast_part(i).wait()

        @pl.loop(0, PIECE)
        def _(row):
            vb[i * PIECE + row] = vf[i % 2, row].astype(BF16)

        if i + 2 < ROWS // PIECE:
            cast_part(i + 2).start()

    def turn(index):
        a[pl.ds(pl.multiple_of(index * OWN, OWN), OWN), :] = at[:, cols(index)].T

    own_act.wait()
    turn(dp)

    @pl.loop(1, 8)
    def _(i):
        far = lax.rem(i, 2)
        q = lax.div(i, 2)
        step = q + lax.div(q, 2) * (1 - 2 * lax.rem(q, 2))
        source = (lax.rem(y_hi + far, 2) * 4 + lax.rem(x + 4 - step, 4)) * 2 + core
        block = at.at[:, cols(source)]
        remote(block, block, act_send, act_recv.at[i - 1], twin).wait_recv()
        remote(block, block, fwd_send, fwd_recv.at[lax.div(source, 2)], twin).start()
        turn(source)

    half_acts = at.at[:, pl.ds(0, TOK // 2)]

    @pl.loop(0, DP // 2)
    def _(i):
        far = lax.rem(i, 2)
        q = lax.div(i, 2)
        step = q + lax.div(q, 2) * (1 - 2 * lax.rem(q, 2))
        origin = lax.rem(y_hi + far, 2) * 4 + lax.rem(x + 4 - step, 4)
        block = at.at[:, cols(origin * 2 + 1 - core)]
        remote(block, block, fwd_send, fwd_recv.at[origin], twin).wait_recv()
        turn(origin * 2 + 1 - core)

    def tokens(step, half):
        return pl.ds(pl.multiple_of(lax.rem(z + step, Z) * BLOCK + half * HALF, HALF), HALF)

    sends = []

    def zsend(c, slot, src, dst, device):
        copy = remote(src, dst, zs_sem.at[c, slot], zr_sem.at[c, slot], device)
        copy.start()
        sends.append(copy)

    def zwait(c, slot, dst):
        remote(dst, dst, zs_sem.at[c, slot], zr_sem.at[c, slot], plus).wait_recv()

    def first(c):
        relayed(0, wr, c)

        @pl.loop(0, WIDTH // 32)
        def _(i):
            rows = pl.ds(pl.multiple_of(i * 32, 32), 32)
            pair = jnp.swapaxes(wr[c, rows], 0, 1)
            wd[c, rows, 0:FC] = pair[0]
            wd[c, rows, FC : 2 * FC] = pair[1]

        @pl.loop(0, 2)
        def _(slot):
            sb[c, slot] = dot(a[tokens(2, slot), :], wd[c]).astype(BF16)

        zsend(c, 0, sb.at[c, 0], rmid.at[c, 0], plus)
        zsend(c, 1, sb.at[c, 1], rmid.at[c, 1], minus)

        @pl.loop(0, 2)
        def _(slot):
            sb[c, 2 + slot] = dot(a[tokens(1 + 2 * slot, 1 - slot), :], wd[c]).astype(BF16)

        zsend(c, 2, sb.at[c, 2], rfin.at[c, 0, 1], plus)
        zsend(c, 3, sb.at[c, 3], rfin.at[c, 1, 0], minus)

    def second(c):
        zwait(c, 0, rmid.at[c, 0])
        zwait(c, 1, rmid.at[c, 1])

        @pl.loop(0, 2)
        def _(slot):
            sb[c, 4 + slot] = (
                dot(a[tokens(1 + 2 * slot, slot), :], wd[c]) + rmid[c, slot].astype(F32)
            ).astype(BF16)

        zsend(c, 4, sb.at[c, 4], rfin.at[c, 0, 0], plus)
        zsend(c, 5, sb.at[c, 5], rfin.at[c, 1, 1], minus)

    def block_sum(c, half):
        return (
            dot(a[tokens(0, half), :], wd[c])
            + rfin[c, 0, half].astype(F32)
            + rfin[c, 1, half].astype(F32)
        )

    def third(c):
        zwait(c, 2, rfin.at[c, 0, 1])
        zwait(c, 3, rfin.at[c, 1, 0])
        zwait(c, 4, rfin.at[c, 0, 0])
        zwait(c, 5, rfin.at[c, 1, 1])
        yls[c] = block_sum(c, 1 - lo).astype(BF16)
        zsend(c, 6, yls.at[c], ylr.at[c], mate)

    def fourth(c):
        zwait(c, 6, ylr.at[c])
        sums = (block_sum(c, lo) + ylr[c].astype(F32)) * width_scale
        gate, up = sums[:, :FC], sums[:, FC:]
        span = slice(c * FC, (c + 1) * FC)
        activated, slope = gelu_parts(gate)
        upstream = cot[:, span].astype(F32)
        hid[:, span] = (activated * up).astype(BF16)
        rows = tokens(0, lo)
        grads[c, rows, 0:FC] = (upstream * up * slope).astype(BF16)
        grads[c, rows, FC : 2 * FC] = (upstream * activated).astype(BF16)
        mine = grads.at[c, rows]
        zsend(c, 7, mine, mine, mate)

    def fifth(c):
        mine = grads.at[c, tokens(0, lo)]
        zsend(c, 8, mine, mine, plus)
        zsend(c, 9, mine, mine, minus)
        theirs = grads.at[c, tokens(0, 1 - lo)]
        zwait(c, 7, theirs)
        zsend(c, 10, theirs, theirs, plus)
        zsend(c, 11, theirs, theirs, minus)

    def sixth(c):
        below, above = grads.at[c, tokens(3, lo)], grads.at[c, tokens(1, 1 - lo)]
        zwait(c, 8, below)
        zsend(c, 12, below, below, plus)
        zwait(c, 11, above)
        zsend(c, 13, above, above, minus)

    def gathered(c):
        zwait(c, 9, grads.at[c, tokens(1, lo)])
        zwait(c, 10, grads.at[c, tokens(3, 1 - lo)])
        zwait(c, 12, grads.at[c, tokens(2, lo)])
        zwait(c, 13, grads.at[c, tokens(2, 1 - lo)])

    def back(c):
        @pl.loop(0, TOK // HALF)
        def _(i):
            rows = pl.ds(pl.multiple_of(i * HALF, HALF), HALF)
            term = lax.dot_general(
                grads[c, rows, :], wd[c], (((1,), (1,)), ((), ())), preferred_element_type=F32
            )
            if c == 0:
                acc[rows, :] = term
            else:
                acc[rows, :] += term

    outs = ((nws, nw), (nms, nm), (nvs, nv))

    def written(c):
        span = pl.ds(c * FC, FC)
        return [
            pltpu.make_async_copy(held, out.at[:, :, span], out_sem.at[i]) for i, (held, out) in enumerate(outs)
        ]

    def weight_grads(c):
        @pl.loop(0, 3)
        def _(i):
            rows = pl.ds(pl.multiple_of(i * 192, 192), 192)
            both = dot(at[rows, :], grads[c]) * width_scale
            gw[0, rows, :] = both[:, :FC]
            gw[1, rows, :] = both[:, FC:]

    def update(c):
        relayed(1, mr, c)
        relayed(2, vr, c)
        if c > 0:
            for copy in written(c - 1):
                copy.wait()

        @pl.loop(0, WIDTH // 32)
        def _(i):
            rows = pl.ds(pl.multiple_of(i * 32, 32), 32)
            mean = jnp.swapaxes(mr[c, rows], 0, 1)
            var = jnp.swapaxes(vr[c, rows], 0, 1)
            for k in range(2):
                grad = gw[k, rows, :]
                moment_one = beta_one * mean[k].astype(F32) + (1.0 - beta_one) * grad
                var_next = beta_two * var[k].astype(F32) + (1.0 - beta_two) * grad * grad
                mean_hat = moment_one * (1.0 / (1.0 - beta_one**RESUME_STEP))
                var_hat = var_next * (1.0 / (1.0 - beta_two**RESUME_STEP))
                master = wd[c, rows, k * FC : (k + 1) * FC].astype(F32)
                updated = master * (1.0 - learn_rate * decay_rate) - learn_rate * mean_hat / (
                    jnp.sqrt(var_hat) + epsilon
                )
                nws[k, rows, :] = updated.astype(BF16)
                nms[k, rows, :] = moment_one.astype(BF16)
                nvs[k, rows, :] = var_next

        for copy in written(c):
            copy.start()

    def stages(step):
        def at_lag(lag):
            return 0 <= step - lag < CH

        if at_lag(0):
            first(step)
        if at_lag(1):
            second(step - 1)
        if step + AHEAD < CH:
            relay(0, w_in, wr, step + AHEAD)
        if at_lag(2):
            third(step - 2)
        if at_lag(3):
            fourth(step - 3)
            relay(1, m_in, mr, step - 3)
        if at_lag(4):
            relay(2, vb, vr, step - 4)
        if at_lag(LAG):
            fifth(step - LAG)
        if at_lag(LAG + 1):
            sixth(step - LAG - 1)
        if at_lag(LAG + 2) and step - LAG - 2 < CH - 1:
            gathered(step - LAG - 2)
            back(step - LAG - 2)
            if step - LAG - 2 < CH - LATE:
                weight_grads(step - LAG - 2)
                update(step - LAG - 2)

    for step in range(CH + LAG + 2):
        stages(step)

    gathered(CH - 1)

    def acc_rows(index):
        return pl.ds(pl.multiple_of(index * OWN, OWN), OWN)

    def swap(j):
        return remote(acc.at[acc_rows(j * 2 + 1 - core)], xr.at[j], x_send.at[j], x_recv.at[j], twin)

    @pl.loop(1, 9)
    def _(i):
        j = peer_line(lax.rem(i, 8))
        rows = pl.ds(pl.multiple_of(j * HALF, HALF), HALF)
        acc[rows, :] += lax.dot_general(
            grads[CH - 1, rows, :], wd[CH - 1], (((1,), (1,)), ((), ())), preferred_element_type=F32
        )
        swap(j).start()

    @pl.loop(1, 9)
    def _(i):
        j = peer_line(lax.rem(i, 8))
        swap(j).wait_recv()
        rows = acc_rows(j * 2 + core)
        total = acc[rows, :] + xr[j]
        acc[rows, :] = total

        @pl.when(i < 8)
        def _():
            xq[i - 1] = total.astype(BF16)
            remote(xq.at[i - 1], xf.at[i - 1], p_send, p_recv, (j * 2 + core, mp)).start()

    for c in range(CH - LATE, CH):
        weight_grads(c)
        update(c)

    pltpu.make_async_copy(xf, xf, p_recv).wait()
    total = acc[acc_rows(dp), :]
    for i in range(7):
        total = total + xf[i].astype(F32)
    ig[...] = (total * width_scale).T.astype(BF16)

    pltpu.make_async_copy(xf, xf, p_send).wait()

    @pl.loop(0, 8)
    def _(j):
        swap(j).wait_send()

    for copy in written(CH - 1):
        copy.wait()
    for copy in sends:
        copy.wait_send()
    for c in range(CH):
        relay_sent(0, wr, c)
        relay_sent(1, mr, c)
        relay_sent(2, vr, c)
    seven = at.at[:, pl.ds(0, 7 * OWN)]
    pltpu.make_async_copy(seven, seven, act_send).wait()
    pltpu.make_async_copy(half_acts, half_acts, fwd_send).wait()


def shards(acts, old_weights, old_mean, old_var, cotangent):
    vmem = pl.BlockSpec(memory_space=pltpu.VMEM)
    hbm = pl.BlockSpec(memory_space=pl.ANY)
    dma = pltpu.SemaphoreType.DMA
    macs = 3 * TOK * WIDTH * 2 * FS

    hidden, input_grad, new_weights, new_mean, new_var = pl.pallas_call(
        kernel,
        out_shape=(
            jax.ShapeDtypeStruct((HALF, FS), BF16),
            jax.ShapeDtypeStruct((WIDTH, OWN), BF16),
            jax.ShapeDtypeStruct((2, WIDTH, FS), BF16),
            jax.ShapeDtypeStruct((2, WIDTH, FS), BF16),
            jax.ShapeDtypeStruct((2, WIDTH, FS), F32),
        ),
        in_specs=[hbm, hbm, hbm, hbm, vmem],
        out_specs=(vmem, vmem, hbm, hbm, hbm),
        scratch_shapes=[
            pltpu.VMEM((2, PIECE, 2, FS * DP), F32),
            pltpu.VMEM((ROWS, 2, FS * DP), BF16),
            pltpu.VMEM((WIDTH, TOK), BF16),
            pltpu.VMEM((TOK, WIDTH), BF16),
            pltpu.VMEM((CH, WIDTH, 2, FC), BF16),
            pltpu.VMEM((CH, WIDTH, 2, FC), BF16),
            pltpu.VMEM((CH, WIDTH, 2, FC), BF16),
            pltpu.VMEM((CH, WIDTH, 2 * FC), BF16),
            pltpu.VMEM((CH, 6, HALF, 2 * FC), BF16),
            pltpu.VMEM((CH, 2, HALF, 2 * FC), BF16),
            pltpu.VMEM((CH, 2, 2, HALF, 2 * FC), BF16),
            pltpu.VMEM((CH, HALF, 2 * FC), BF16),
            pltpu.VMEM((CH, HALF, 2 * FC), BF16),
            pltpu.VMEM((CH, TOK, 2 * FC), BF16),
            pltpu.VMEM((TOK, WIDTH), F32),
            pltpu.VMEM((2, WIDTH, FC), F32),
            pltpu.VMEM((2, WIDTH, FC), BF16),
            pltpu.VMEM((2, WIDTH, FC), BF16),
            pltpu.VMEM((2, WIDTH, FC), F32),
            pltpu.VMEM((8, OWN, WIDTH), F32),
            pltpu.VMEM((7, OWN, WIDTH), BF16),
            pltpu.VMEM((7, OWN, WIDTH), BF16),
            dma, dma((2,)), dma((3,)), dma, dma((7,)), dma, dma((DP // 2,)), dma((3, CH)), dma((3, CH)),
            dma((CH, 14)), dma((CH, 14)), dma((8,)), dma((8,)), dma, dma,
        ],
        compiler_params=pltpu.CompilerParams(
            collective_id=0, has_side_effects=True, vmem_limit_bytes=63 * 2**20
        ),
        cost_estimate=pl.CostEstimate(flops=2 * macs, bytes_accessed=40 * 2**20, transcendentals=0),
    )(
        acts.T,
        jnp.transpose(old_weights, (1, 0, 2)),
        jnp.transpose(old_mean, (1, 0, 2)),
        jnp.transpose(old_var, (1, 0, 2)),
        cotangent,
    )
    return hidden, input_grad.T, new_weights, new_mean, new_var


def solution(mesh):
    placed = (
        P("dp", "mp"),
        P(None, ("mp", "dp"), None),
        P(None, ("mp", "dp"), None),
        P(None, ("mp", "dp"), None),
        P("mp", "dp"),
    )
    return jax.shard_map(
        shards,
        mesh=mesh,
        in_specs=placed,
        out_specs=(
            P("mp", "dp"),
            P("dp", "mp"),
            P(None, "mp", "dp"),
            P(None, "mp", "dp"),
            P(None, "mp", "dp"),
        ),
        check_vma=False,
    )
```
